512 devices in a mesh: freq: 32 (over y, x, core), src: 2 (over z_hi), rcv: 8 (over z_lo).
Axes of the slice: x: 4, y: 4, z: 16 (z_hi: 2, z_lo: 8; z = z_hi * 8 + z_lo), core: 2. Of those that a mesh axis runs over, the one named last changes fastest.
Arguments:
- packets: bfloat16 [1048576, 256], P(('freq', 'src', 'rcv')), parts along dimension 0, may hold values from -6 to 6
- packet_bin: int32 [1048576], P(('freq', 'src', 'rcv')), parts along dimension 0, may hold values from 0 to 32767, as said below
- obliquity: bfloat16 [65536], P(('freq', 'src')), parts along dimension 0, may hold values from 0.0066223145 to 0.06591797
- wavelet: float32 [64], P('freq'), parts along dimension 0, may hold values from 0.5 to 1.5
Outputs:
- multiples: float32 [2, 65536, 2048], P(None, ('freq', 'src'), 'rcv'), parts along dimension 1
The draws below stay inside these ranges and needn't reach their ends.
There are 32 independent parts, one for each index of `freq`. The reference program is written for one: setup_inputs(seed, part) draws one part's arguments, and reference() takes and returns one part's arrays. A program takes and returns all parts, laid end to end along the dimension named above; each array names one. Nothing has to cross between parts.
Inputs may be any that keep to these rules, and one draw needn't show every extreme that they name: `packet_bin`: within one part every bin id appears exactly once over all devices' lists. The owner of bin s * 16 + c is the device with src index s // (2048 // 2) and rcv index c // (2048 // 8 // 128). One device's list holds at most 256 bins of any one owner; every device holds exactly 256 bins of one owner, and every owner receives exactly 256 bins from one device.
All inputs are finite; a program needn't handle non-finite values.
Results may differ from the reference program's by a relative error of at most 0.0029.
Values may be sent and summed in bfloat16 or wider, within the bound.
A program may use at most 64 MiB of HBM per device.

```python
import math
import jax
import jax.numpy as jnp

N = 2048
RB = 128
GROUP = 16
PK = 2048
CAP = 256
N_SRC = 2
N_RCV = 8


def draw_packet_bin(key, part):
    key = jax.random.fold_in(key, 11)
    key_units, key_shift, key_slots, key_order = jax.random.split(key, 4)
    grid_size = N_SRC * N_RCV
    unit_draws = jax.random.randint(key_units, (grid_size - 1,), 2, 5).astype(jnp.int32)
    unit_total = jnp.sum(unit_draws)
    run_bounds = (PK - CAP) * jnp.cumsum(unit_draws) // unit_total
    rest_counts = jnp.diff(jnp.concatenate([jnp.zeros((1,), jnp.int32), run_bounds.astype(jnp.int32)]))
    pair_weights = jnp.concatenate([jnp.full((1,), CAP, jnp.int32), rest_counts])
    sender_shift = jax.random.permutation(key_shift, grid_size).astype(jnp.int32)
    owners = jnp.arange(grid_size, dtype=jnp.int32)
    pair_counts = pair_weights[(owners[None, :] - sender_shift[:, None]) % grid_size]
    running_sum = jnp.cumsum(pair_counts, axis=0)
    positions = jnp.arange(PK, dtype=jnp.int32)
    sender_of = jnp.sum((running_sum[:, :, None] <= positions[None, None, :]).astype(jnp.int32), axis=0)
    slot_keys = jax.random.split(key_slots, grid_size)

    def owner_slots(sub_key):
        return jax.random.permutation(sub_key, PK).astype(jnp.int32)
    slot_perms = jax.vmap(owner_slots)(slot_keys)
    rows_dev = N // N_SRC
    blocks_dev = N // N_RCV // RB
    source = owners[:, None] // N_RCV * rows_dev + slot_perms // blocks_dev
    recv_block = owners[:, None] % N_RCV * blocks_dev + slot_perms % blocks_dev
    bin_ids = source * (N // RB) + recv_block
    tie_break = jax.random.permutation(key_order, grid_size * PK).astype(jnp.int32)
    sort_keys = sender_of.reshape(-1) * (grid_size * PK) + tie_break
    acquisition = jnp.argsort(sort_keys, stable=True)
    return bin_ids.reshape(-1)[acquisition].astype(jnp.int32)


def block_levels(rng, dims, cuts, low, high):
    def one(dim, shards_of):
        draws = jax.random.uniform(jax.random.fold_in(jax.random.fold_in(rng, 6), dim), (shards_of,), jnp.float32, low / len(cuts), high / len(cuts))
        return jnp.repeat(jnp.exp(draws), dims[dim] // shards_of).reshape((-1,) + (1,) * (len(dims) - dim - 1))

    loudness = one(*cuts[0])
    for cut in cuts[1:]:
        loudness = loudness * one(*cut)
    return loudness


def scatter_about(rng, extent, deviation, limit, pieces=(), held_as=jnp.bfloat16):
    drawn = deviation * jax.random.normal(rng, extent, jnp.float32)
    if pieces:
        drawn = drawn * block_levels(rng, extent, pieces, -0.22, 0.18)
    return jnp.clip(drawn, -limit, limit).astype(held_as)


def setup_inputs(seed: int = 0, part: int = 0) -> dict:
    splits = jax.random.split(jax.random.key(seed), 5)
    part_keys = jax.random.split(jax.random.fold_in(splits[4], part), 5)
    return {
        "packets": scatter_about(part_keys[0], (GROUP * PK, 2 * RB), 1.0, 6.0, ((0, 16),)),
        "packet_bin": draw_packet_bin(jax.random.fold_in(jax.random.fold_in(splits[4], part), 71), part),
        "obliquity": jnp.clip(jnp.exp(math.log(0.06591797) - 2.29796615 * jax.random.uniform(part_keys[2], (N,), jnp.float32) ** block_levels(part_keys[2], (N,), ((0, 2),), -0.2, 0.2)), 0.0066223145, 0.06591797).astype(jnp.bfloat16),
        "wavelet": jnp.clip(jax.random.uniform(part_keys[3], (2,), jnp.float32, 0.5, 1.5), 0.5, 1.5),
    }


def reference(packets, packet_bin, obliquity, wavelet):
    total_blocks = N // RB
    binned = jnp.zeros((N * total_blocks, 2 * RB), jnp.bfloat16).at[packet_bin].set(packets)
    data_matrix = binned.reshape(N, total_blocks, 2, RB).transpose(2, 0, 1, 3).reshape(2, N, N)
    real_part = data_matrix[0].astype(jnp.float32)
    imag_part = data_matrix[1].astype(jnp.float32)
    obl_scale = obliquity.astype(jnp.float32)[:, None]
    filt_real = ((wavelet[0] * real_part - wavelet[1] * imag_part) * obl_scale).astype(jnp.bfloat16)
    filt_imag = ((wavelet[0] * imag_part + wavelet[1] * real_part) * obl_scale).astype(jnp.bfloat16)
    multiple_real = jnp.dot(data_matrix[0], filt_real, preferred_element_type=jnp.float32) - jnp.dot(data_matrix[1], filt_imag, preferred_element_type=jnp.float32)
    multiple_imag = jnp.dot(data_matrix[0], filt_imag, preferred_element_type=jnp.float32) + jnp.dot(data_matrix[1], filt_real, preferred_element_type=jnp.float32)
    return jnp.stack([multiple_real, multiple_imag])
```

```python
import functools

import jax
import jax.numpy as jnp
from jax import lax
from jax.experimental import pallas as pl
from jax.experimental.pallas import tpu as pltpu
from jax.sharding import PartitionSpec as P

MESH = pl.DeviceIdType.MESH
N = 2048
RB = 128
BLOCKS = N // RB
GROUP = 16
HALF = N // 2
PK = 2048
WIDTH = 2 * RB
SUB = 4
ROWS = PK // SUB
FAR = GROUP // 2
WIN = 384
PANELS = BLOCKS + 2
BF16 = jnp.bfloat16
F32 = jnp.float32


def kernel(rows_ref, bins_ref, obl_in_ref, wave_ref, out_ref, *scratch):
    bufs, scratch = scratch[:16], scratch[16:]
    auxs, scratch = scratch[:16], scratch[16:]
    tabs, scratch = scratch[:16], scratch[16:]
    (panel, weights, onehot, key_cols, key_rows, rank_rows, digits, obl, send_sem, recv_sem,
     aux_send, aux_recv, tab_sem, obl_sem) = scratch

    src, rcv = lax.axis_index("src"), lax.axis_index("rcv")
    me = src * (GROUP // 2) + rcv

    def device(rank):
        rank = lax.rem(rank + GROUP, GROUP)
        return {"src": rank // (GROUP // 2), "rcv": lax.rem(rank, GROUP // 2)}

    ahead = (device(me + 1), device(me - 1))
    partner = device(me + FAR)

    def place(d, t):
        if t == 0:
            return 0
        if t == FAR:
            return 15
        return t if d == 0 else t + 7

    def carried(d, t, s):
        return t < FAR - 1 or (s < SUB // 2) == (d == 0)

    def data_copy(d, t, s):
        part = pl.ds(s * ROWS, ROWS)
        return pltpu.make_async_remote_copy(
            src_ref=bufs[place(d, t)].at[part],
            dst_ref=bufs[place(d, t + 1)].at[part],
            send_sem=send_sem.at[d, t, s],
            recv_sem=recv_sem.at[d, t, s],
            device_id=ahead[d],
            device_id_type=MESH,
        )

    def aux_copy(d, t):
        return pltpu.make_async_remote_copy(
            src_ref=auxs[place(d, t)],
            dst_ref=auxs[place(d, t + 1)],
            send_sem=aux_send.at[d, t],
            recv_sem=aux_recv.at[d, t],
            device_id=ahead[d],
            device_id_type=MESH,
        )

    def table_copy(i):
        return pltpu.make_async_copy(auxs[i].at[pl.ds(16, 8)], tabs[i], tab_sem.at[i])

    obl_copy = pltpu.make_async_remote_copy(
        src_ref=obl.at[0],
        dst_ref=obl.at[1],
        send_sem=obl_sem.at[0],
        recv_sem=obl_sem.at[1],
        device_id=partner,
        device_id_type=MESH,
    )

    barrier = pltpu.get_barrier_semaphore()
    for other in (*ahead, partner):
        pl.semaphore_signal(barrier, inc=1, device_id=other, device_id_type=MESH)

    bins = bins_ref[...]
    keys = ((bins >> 14) << 14) + ((bins & 15) << 10) + ((bins >> 4) & 1023)
    key_rows[...] = keys
    digits[...] = jnp.zeros_like(digits)
    high, low = (keys >> 7).astype(F32), (keys & 127).astype(F32)
    for i in range(BLOCKS):
        lanes = slice(i * RB, (i + 1) * RB)
        digits[0:1, lanes] = high[i : i + 1, :]
        digits[1:2, lanes] = low[i : i + 1, :]
        key_cols[i * RB : (i + 1) * RB, :] = jnp.broadcast_to(key_rows[i : i + 1, :], (RB, RB)).T

    def rank_block(i, _):
        mine = jnp.broadcast_to(key_rows[pl.ds(i, 1), :], (RB, RB))
        total = jnp.zeros((RB, RB), jnp.int32)
        for j in range(BLOCKS):
            total += jnp.where(key_cols[j * RB : (j + 1) * RB, :] < mine, 1, 0)
        rank_rows[pl.ds(i, 1), :] = jnp.sum(total, axis=0, keepdims=True)
        return 0

    lax.fori_loop(0, BLOCKS, rank_block, 0)
    obl[0] = obl_in_ref[...]
    pl.semaphore_wait(barrier, 3)
    obl_copy.start()

    two_digits = digits[...].astype(BF16)
    for s in range(SUB):
        slots = lax.broadcasted_iota(jnp.int32, (ROWS, RB), 0) + s * ROWS
        for i in range(BLOCKS):
            onehot[:, i * RB : (i + 1) * RB] = jnp.where(
                slots == rank_rows[i : i + 1, :], 1.0, 0.0
            ).astype(BF16)
        taken = onehot[...]
        bufs[0][s * ROWS : (s + 1) * ROWS, :] = jnp.dot(
            taken, rows_ref[...], preferred_element_type=F32
        ).astype(BF16)
        for d in (0, 1):
            data_copy(d, 0, s).start()
        found = lax.dot_general(
            two_digits, taken, (((1,), (1,)), ((), ())), preferred_element_type=F32
        )
        found = (found[0:1, :] * 128.0 + found[1:2, :]).astype(jnp.int32)
        per = ROWS // RB
        for i in range(per):
            auxs[0][s * per + i : s * per + i + 1, :] = found[:, i * RB : (i + 1) * RB]
    starts = lax.broadcasted_iota(jnp.int32, (RB, RB), 1) * HALF
    total = jnp.zeros((RB, RB), jnp.int32)
    for j in range(BLOCKS):
        total += jnp.where(key_cols[j * RB : (j + 1) * RB, :] < starts, 1, 0)
    offsets = jnp.sum(total, axis=0, keepdims=True)
    auxs[0][16:24, :] = jnp.broadcast_to(offsets, (8, RB))
    for d in (0, 1):
        aux_copy(d, 0).start()
    table_copy(0).start()
    table_copy(0).wait()

    slot_ids = lax.broadcasted_iota(jnp.int32, (HALF, RB), 0)

    def bucket(lists, first, j, _):
        b = jnp.where(j < BLOCKS, src * BLOCKS + j, (1 - src) * BLOCKS + rcv * 2 + j - BLOCKS)
        hits, packets = [], []
        for i in lists:
            k = jnp.clip(tabs[i][0, b] // RB, 0, (PK - WIN) // RB)
            for w in range(WIN // RB):
                ids = auxs[i][pl.ds(k + w, 1), :] - b * HALF
                hits.append(jnp.where(slot_ids == ids, 1.0, 0.0).astype(BF16))
            packets.append(bufs[i][pl.ds(k * RB, WIN), :])
        taken = jnp.concatenate(hits, axis=1)
        found = packets[0] if len(packets) == 1 else jnp.concatenate(packets, axis=0)
        placed = jnp.dot(taken, found, preferred_element_type=F32).astype(BF16)
        lanes = pl.ds(pl.multiple_of(j * WIDTH, WIDTH), WIDTH)
        if first:
            panel[:, lanes] = placed
        else:
            panel[:, lanes] += placed
        return 0

    def buckets(lists, first, low, high):
        lax.fori_loop(low, high, functools.partial(bucket, lists, first), 0)

    edges = [PANELS * s // SUB for s in range(SUB + 1)]
    for t in range(FAR):
        lists = (0,) if t == 0 else (place(0, t), place(1, t))
        for s in range(SUB):
            for d in (0, 1):
                if carried(d, t, s):
                    data_copy(d, t, s).wait_recv()
                    if t + 1 < FAR and carried(d, t + 1, s):
                        data_copy(d, t + 1, s).start()
            if s == SUB - 1:
                for d in (0, 1):
                    if t + 1 < FAR or d == 0:
                        aux_copy(d, t).wait_recv()
                        i = place(d, t + 1)
                        table_copy(i).start()
                        if t + 2 < FAR or (t + 2 == FAR and d == 0):
                            aux_copy(d, t + 1).start()
                for d in (0, 1):
                    if t + 1 < FAR or d == 0:
                        table_copy(place(d, t + 1)).wait()
            buckets(lists, t == 0, edges[s], edges[s + 1])
    buckets((15,), False, 0, PANELS)

    obl_copy.wait()
    w0, w1 = wave_ref[0], wave_ref[1]

    def filter_block(c, _):
        here = c // (BLOCKS // 2) == src
        lane = jnp.where(here, rcv * 2 * WIDTH, BLOCKS * WIDTH)
        block = lax.rem(c, BLOCKS // 2)
        data = panel[
            pl.ds(pl.multiple_of(block * RB, RB), RB),
            pl.ds(pl.multiple_of(lane, 2 * WIDTH), 2 * WIDTH),
        ].astype(F32)
        row = obl[jnp.where(here, 0, 1), pl.ds(block, 1), :]
        scale = jnp.broadcast_to(row, (RB, RB)).T
        for i in range(2):
            re = data[:, i * WIDTH : i * WIDTH + RB]
            im = data[:, i * WIDTH + RB : (i + 1) * WIDTH]
            filt_re = ((w0 * re - w1 * im) * scale).astype(BF16)
            filt_im = ((w0 * im + w1 * re) * scale).astype(BF16)
            k = pl.multiple_of(c * WIDTH, WIDTH)
            left, right = slice(i * RB, (i + 1) * RB), slice(WIDTH + i * RB, WIDTH + (i + 1) * RB)
            weights[pl.ds(k, RB), left] = filt_re
            weights[pl.ds(k, RB), right] = filt_im
            weights[pl.ds(k + RB, RB), left] = -filt_im
            weights[pl.ds(k + RB, RB), right] = filt_re
        return 0

    lax.fori_loop(0, BLOCKS, filter_block, 0)

    tile = 512

    def product(m, _):
        part = pl.ds(pl.multiple_of(m * tile, tile), tile)
        for i in range(2):
            out_ref[i, part, :] = jnp.dot(
                panel[part, : BLOCKS * WIDTH],
                weights[:, i * WIDTH : (i + 1) * WIDTH],
                preferred_element_type=F32,
            )
        return 0

    lax.fori_loop(0, HALF // tile, product, 0)

    for t in range(FAR):
        for d in (0, 1):
            for s in range(SUB):
                if carried(d, t, s):
                    data_copy(d, t, s).wait_send()
            if t + 1 < FAR or d == 0:
                aux_copy(d, t).wait_send()


def on_device(packets, packet_bin, obliquity, wavelet):
    vmem = pl.BlockSpec(memory_space=pltpu.VMEM)
    dma = pltpu.SemaphoreType.DMA
    return pl.pallas_call(
        kernel,
        out_shape=jax.ShapeDtypeStruct((2, HALF, WIDTH), F32),
        in_specs=[vmem, vmem, vmem, pl.BlockSpec(memory_space=pltpu.SMEM)],
        out_specs=vmem,
        scratch_shapes=[
            *[pltpu.VMEM((PK, WIDTH), BF16)] * 16,
            *[pltpu.VMEM((24, RB), jnp.int32)] * 16,
            *[pltpu.SMEM((8, RB), jnp.int32)] * 16,
            pltpu.VMEM((HALF, PANELS * WIDTH), BF16),
            pltpu.VMEM((BLOCKS * WIDTH, 2 * WIDTH), BF16),
            pltpu.VMEM((ROWS, PK), BF16),
            pltpu.VMEM((PK, RB), jnp.int32),
            pltpu.VMEM((BLOCKS, RB), jnp.int32),
            pltpu.VMEM((BLOCKS, RB), jnp.int32),
            pltpu.VMEM((8, PK), F32),
            pltpu.VMEM((2, 8, RB), F32),
            dma((2, FAR, SUB)),
            dma((2, FAR, SUB)),
            dma((2, FAR)),
            dma((2, FAR)),
            dma((16,)),
            dma((2,)),
        ],
        compiler_params=pltpu.CompilerParams(
            collective_id=0, has_side_effects=True, vmem_limit_bytes=56 << 20
        ),
    )(
        packets,
        packet_bin.reshape(BLOCKS, RB),
        obliquity.astype(F32).reshape(8, RB),
        wavelet,
    )


def solution(mesh):
    return jax.shard_map(
        on_device,
        mesh=mesh,
        in_specs=(
            P(("freq", "src", "rcv"), None),
            P(("freq", "src", "rcv")),
            P(("freq", "src")),
            P("freq"),
        ),
        out_specs=P(None, ("freq", "src"), "rcv"),
        check_vma=False,
    )
```

```python
import functools

import jax
import jax.numpy as jnp
from jax import lax
from jax.experimental import pallas as pl
from jax.experimental.pallas import tpu as pltpu
from jax.sharding import PartitionSpec as P

MESH = pl.DeviceIdType.MESH
N = 2048
RB = 128
BLOCKS = N // RB
GROUP = 16
HALF = N // 2
PK = 2048
WIDTH = 2 * RB
SUB = 4
ROWS = PK // SUB
FAR = GROUP // 2
WIN = 384
PANELS = BLOCKS + 2
PAIR, ONE = 3, 6
BF16 = jnp.bfloat16
F32 = jnp.float32


def kernel(rows_ref, bins_ref, obl_in_ref, wave_ref, out_ref, lists, auxs, tabs, now, now_aux, panel, weights,
           slots16, onehot, key_cols, key_rows, rank_rows, digits, obl, send_sem, recv_sem, aux_send, aux_recv,
           obl_send, obl_recv, tab_sem):
    src, rcv = lax.axis_index("src"), lax.axis_index("rcv")
    me = src * FAR + rcv

    def device(rank):
        rank = lax.rem(rank + GROUP, GROUP)
        return {"src": rank // FAR, "rcv": lax.rem(rank, FAR)}

    ahead = (device(me + 1), device(me - 1))

    def place(d, t):
        if d == 0:
            return t
        if isinstance(t, int):
            return t if t in (0, FAR) else t + FAR
        return jnp.where(lax.rem(t, FAR) == 0, t, t + FAR)

    def data_copy(d, t, s):
        part = pl.ds(s * ROWS, ROWS)
        return pltpu.make_async_remote_copy(
            src_ref=lists.at[place(d, t), part],
            dst_ref=lists.at[place(d, t + 1), part],
            send_sem=send_sem.at[d, t, s],
            recv_sem=recv_sem.at[d, t, s],
            device_id=ahead[d],
            device_id_type=MESH,
        )

    def aux_copy(d, t):
        return pltpu.make_async_remote_copy(
            src_ref=auxs.at[place(d, t)],
            dst_ref=auxs.at[place(d, t + 1)],
            send_sem=aux_send.at[d, t],
            recv_sem=aux_recv.at[d, t],
            device_id=ahead[d],
            device_id_type=MESH,
        )

    def obl_copy(t):
        return pltpu.make_async_remote_copy(
            src_ref=obl.at[t],
            dst_ref=obl.at[t + 1],
            send_sem=obl_send.at[t],
            recv_sem=obl_recv.at[t],
            device_id=ahead[0],
            device_id_type=MESH,
        )

    def table_copy(i):
        return pltpu.make_async_copy(auxs.at[i, pl.ds(BLOCKS, 8)], tabs.at[i], tab_sem.at[i])

    barrier = pltpu.get_barrier_semaphore()
    for other in ahead:
        pl.semaphore_signal(barrier, inc=1, device_id=other, device_id_type=MESH)

    bins = bins_ref[...]
    keys = ((bins >> 14) << 14) + ((bins & 15) << 10) + ((bins >> 4) & 1023)
    key_rows[...] = keys
    digits[...] = jnp.zeros_like(digits)
    high, low = (keys >> 7).astype(F32), (keys & 127).astype(F32)
    for i in range(BLOCKS):
        lanes = slice(i * RB, (i + 1) * RB)
        digits[0:1, lanes] = high[i : i + 1, :]
        digits[1:2, lanes] = low[i : i + 1, :]
        key_cols[i * RB : (i + 1) * RB, :] = jnp.broadcast_to(key_rows[i : i + 1, :], (RB, RB)).T

    def rank_block(i, _):
        mine = jnp.broadcast_to(key_rows[pl.ds(i, 1), :], (RB, RB))
        total = jnp.zeros((RB, RB), jnp.int32)
        for j in range(BLOCKS):
            total += jnp.where(key_cols[j * RB : (j + 1) * RB, :] < mine, 1, 0)
        rank_rows[pl.ds(i, 1), :] = jnp.sum(total, axis=0, keepdims=True)
        return 0

    lax.fori_loop(0, BLOCKS, rank_block, 0)
    obl[0] = obl_in_ref[...]
    pl.semaphore_wait(barrier, 2)

    two_digits = digits[...].astype(BF16)
    for s in range(SUB):
        slots = lax.broadcasted_iota(jnp.int32, (ROWS, RB), 0) + s * ROWS
        for i in range(BLOCKS):
            onehot[:, i * RB : (i + 1) * RB] = jnp.where(
                slots == rank_rows[i : i + 1, :], 1.0, 0.0
            ).astype(BF16)
        taken = onehot[...]
        lists[0, s * ROWS : (s + 1) * ROWS, :] = jnp.dot(
            taken, rows_ref[...], preferred_element_type=F32
        ).astype(BF16)
        for d in (0, 1):
            data_copy(d, 0, s).start()
        found = lax.dot_general(
            two_digits, taken, (((1,), (1,)), ((), ())), preferred_element_type=F32
        )
        found = (found[0:1, :] * 128.0 + found[1:2, :]).astype(jnp.int32)
        per = ROWS // RB
        for i in range(per):
            auxs[0, s * per + i : s * per + i + 1, :] = found[:, i * RB : (i + 1) * RB]
    starts = lax.broadcasted_iota(jnp.int32, (RB, RB), 1) * HALF
    total = jnp.zeros((RB, RB), jnp.int32)
    for j in range(BLOCKS):
        total += jnp.where(key_cols[j * RB : (j + 1) * RB, :] < starts, 1, 0)
    offsets = jnp.sum(total, axis=0, keepdims=True)
    auxs[0, BLOCKS:, :] = jnp.broadcast_to(offsets, (8, RB))
    for d in (0, 1):
        aux_copy(d, 0).start()
    obl_copy(0).start()
    table_copy(0).start()
    table_copy(0).wait()

    slot_ids = lax.broadcasted_iota(jnp.int32, (HALF // 16, 16, RB), 0) * 16
    slot_ids = (slot_ids + lax.broadcasted_iota(jnp.int32, (HALF // 16, 16, RB), 1)).astype(jnp.int16)
    slots16[...] = slot_ids
    panel[...] = jnp.zeros_like(panel)

    def take(i, slot):
        def some(r, _):
            part = pl.ds(r * WIDTH, WIDTH)
            now[i, part, :] = lists[slot, part, :]
            return 0

        lax.fori_loop(0, PK // WIDTH, some, 0)
        now_aux[i] = auxs[slot, :BLOCKS, :]

    def place_rows(slots, count, g, _):
        placed = []
        for j in [g * count + i for i in range(count)]:
            b = jnp.where(j < BLOCKS, src * BLOCKS + j, (1 - src) * BLOCKS + rcv * 2 + j - BLOCKS)
            hits, packets = [], []
            for i, slot in enumerate(slots):
                k = jnp.clip(tabs[slot, 0, b] // RB, 0, (PK - WIN) // RB)
                for w in range(WIN // RB):
                    ids = now_aux[i, pl.ds(k + w, 1), :] - b * HALF
                    ids = jnp.broadcast_to(ids, (16, RB)).astype(jnp.int16)
                    hit = jnp.where(slots16[...] == ids[None], jnp.ones((), BF16), jnp.zeros((), BF16))
                    hits.append(hit.reshape(HALF, RB))
                packets.append(now[i, pl.ds(k * RB, WIN), :])
            found = packets[0] if len(packets) == 1 else jnp.concatenate(packets, axis=0)
            placed.append(
                jnp.dot(jnp.concatenate(hits, axis=1), found, preferred_element_type=F32).astype(BF16)
            )
        lanes = pl.ds(pl.multiple_of(g * (count * WIDTH), count * WIDTH), count * WIDTH)
        panel[:, lanes] += jnp.concatenate(placed, axis=1)
        return 0

    def step(t, _):
        slots = (t, place(1, t))
        take(0, slots[0])
        take(1, slots[1])

        @pl.when(t == 0)
        def _():
            now_aux[1] = jnp.full((BLOCKS, RB), -1, jnp.int32)

        def sub_block(s, _):
            groups = PANELS // PAIR
            lax.fori_loop(
                groups * s // SUB, groups * (s + 1) // SUB, functools.partial(place_rows, slots, PAIR), 0
            )

            @pl.when(t < FAR - 1)
            def _():
                for d in (0, 1):
                    data_copy(d, t, s).wait_recv()

                    @pl.when((t < FAR - 2) | ((s < SUB // 2) == (d == 0)))
                    def _(d=d):
                        data_copy(d, t + 1, s).start()

            return 0

        lax.fori_loop(0, SUB, sub_block, 0)

        @pl.when(t < FAR - 1)
        def _():
            for d in (0, 1):
                aux_copy(d, t).wait_recv()
                table_copy(place(d, t + 1)).start()
            aux_copy(0, t + 1).start()

            @pl.when(t < FAR - 2)
            def _():
                aux_copy(1, t + 1).start()

            obl_copy(t).wait_recv()
            obl_copy(t + 1).start()
            for d in (0, 1):
                table_copy(place(d, t + 1)).wait()

        return 0

    lax.fori_loop(0, FAR, step, 0)
    aux_copy(0, FAR - 1).wait_recv()
    table_copy(FAR).start()
    for s in range(SUB):
        data_copy(int(s >= SUB // 2), FAR - 1, s).wait_recv()
    take(0, FAR)
    table_copy(FAR).wait()
    lax.fori_loop(0, PANELS // ONE, functools.partial(place_rows, (FAR,), ONE), 0)

    obl_copy(FAR - 1).wait_recv()
    w0, w1 = wave_ref[0], wave_ref[1]

    def filter_block(c, _):
        here = c // (BLOCKS // 2) == src
        lane = jnp.where(here, rcv * 2 * WIDTH, BLOCKS * WIDTH)
        block = lax.rem(c, BLOCKS // 2)
        data = panel[
            pl.ds(pl.multiple_of(block * RB, RB), RB),
            pl.ds(pl.multiple_of(lane, 2 * WIDTH), 2 * WIDTH),
        ].astype(F32)
        row = obl[jnp.where(here, 0, FAR), pl.ds(block, 1), :]
        scale = jnp.broadcast_to(row, (RB, RB)).T
        for i in range(2):
            re = data[:, i * WIDTH : i * WIDTH + RB]
            im = data[:, i * WIDTH + RB : (i + 1) * WIDTH]
            filt_re = ((w0 * re - w1 * im) * scale).astype(BF16)
            filt_im = ((w0 * im + w1 * re) * scale).astype(BF16)
            k = pl.multiple_of(c * WIDTH, WIDTH)
            left, right = slice(i * RB, (i + 1) * RB), slice(WIDTH + i * RB, WIDTH + (i + 1) * RB)
            weights[pl.ds(k, RB), left] = filt_re
            weights[pl.ds(k, RB), right] = filt_im
            weights[pl.ds(k + RB, RB), left] = -filt_im
            weights[pl.ds(k + RB, RB), right] = filt_re
        return 0

    lax.fori_loop(0, BLOCKS, filter_block, 0)

    tile = 512

    def product(m, _):
        part = pl.ds(pl.multiple_of(m * tile, tile), tile)
        for i in range(2):
            out_ref[i, part, :] = jnp.dot(
                panel[part, : BLOCKS * WIDTH],
                weights[:, i * WIDTH : (i + 1) * WIDTH],
                preferred_element_type=F32,
            )
        return 0

    lax.fori_loop(0, HALF // tile, product, 0)

    def sent(t, _):
        for d in (0, 1):
            for s in range(SUB):

                @pl.when((t < FAR - 1) | ((s < SUB // 2) == (d == 0)))
                def _(d=d, s=s):
                    data_copy(d, t, s).wait_send()

        aux_copy(0, t).wait_send()
        obl_copy(t).wait_send()

        @pl.when(t < FAR - 1)
        def _():
            aux_copy(1, t).wait_send()

        return 0

    lax.fori_loop(0, FAR, sent, 0)


def on_device(packets, packet_bin, obliquity, wavelet):
    vmem = pl.BlockSpec(memory_space=pltpu.VMEM)
    dma = pltpu.SemaphoreType.DMA
    return pl.pallas_call(
        kernel,
        out_shape=jax.ShapeDtypeStruct((2, HALF, WIDTH), F32),
        in_specs=[vmem, vmem, vmem, pl.BlockSpec(memory_space=pltpu.SMEM)],
        out_specs=vmem,
        scratch_shapes=[
            pltpu.VMEM((GROUP, PK, WIDTH), BF16),
            pltpu.VMEM((GROUP, 24, RB), jnp.int32),
            pltpu.SMEM((GROUP, 8, RB), jnp.int32),
            pltpu.VMEM((2, PK, WIDTH), BF16),
            pltpu.VMEM((2, BLOCKS, RB), jnp.int32),
            pltpu.VMEM((HALF, PANELS * WIDTH), BF16),
            pltpu.VMEM((BLOCKS * WIDTH, 2 * WIDTH), BF16),
            pltpu.VMEM((HALF // 16, 16, RB), jnp.int16),
            pltpu.VMEM((ROWS, PK), BF16),
            pltpu.VMEM((PK, RB), jnp.int32),
            pltpu.VMEM((BLOCKS, RB), jnp.int32),
            pltpu.VMEM((BLOCKS, RB), jnp.int32),
            pltpu.VMEM((8, PK), F32),
            pltpu.VMEM((FAR + 1, 8, RB), F32),
            dma((2, FAR, SUB)),
            dma((2, FAR, SUB)),
            dma((2, FAR)),
            dma((2, FAR)),
            dma((FAR,)),
            dma((FAR,)),
            dma((GROUP,)),
        ],
        compiler_params=pltpu.CompilerParams(
            collective_id=0, has_side_effects=True, vmem_limit_bytes=46 << 20
        ),
    )(
        packets,
        packet_bin.reshape(BLOCKS, RB),
        obliquity.astype(F32).reshape(8, RB),
        wavelet,
    )


def solution(mesh):
    return jax.shard_map(
        on_device,
        mesh=mesh,
        in_specs=(
            P(("freq", "src", "rcv"), None),
            P(("freq", "src", "rcv")),
            P(("freq", "src")),
            P("freq"),
        ),
        out_specs=P(None, ("freq", "src"), "rcv"),
        check_vma=False,
    )
```

```python
import functools

import jax
import jax.numpy as jnp
from jax import lax
from jax.experimental import pallas as pl
from jax.experimental.pallas import tpu as pltpu
from jax.sharding import PartitionSpec as P

MESH = pl.DeviceIdType.MESH
N = 2048
RB = 128
BLOCKS = N // RB
GROUP = 16
HALF = N // 2
PK = 2048
WIDTH = 2 * RB
SUB = 4
ROWS = PK // SUB
FAR = GROUP // 2
WIN = 384
PANELS = BLOCKS + 2
PAIR, ONE = 3, 6
BF16 = jnp.bfloat16
F32 = jnp.float32


def kernel(rows_hbm, bins_hbm, obl_in_ref, wave_hbm, out_ref, rows_ref, bins_ref, wave_ref, lists, auxs, offs, tabs,
           now, now_aux, panel, weights, slots16, onehot, key_cols, key_rows, rank_rows, digits, obl, send_sem,
           recv_sem, aux_send, aux_recv, off_send, off_recv, obl_send, obl_recv, tab_sem, in_sem):
    bins_in = pltpu.make_async_copy(bins_hbm, bins_ref, in_sem.at[0])
    rows_in = pltpu.make_async_copy(rows_hbm, rows_ref, in_sem.at[1])
    wave_in = pltpu.make_async_copy(wave_hbm, wave_ref, in_sem.at[2])
    for copy in (bins_in, rows_in, wave_in):
        copy.start()
    src, rcv = lax.axis_index("src"), lax.axis_index("rcv")
    me = src * FAR + rcv

    def device(rank):
        rank = lax.rem(rank + GROUP, GROUP)
        return {"src": rank // FAR, "rcv": lax.rem(rank, FAR)}

    ahead = (device(me + 1), device(me - 1))

    def place(d, t):
        if d == 0:
            return t
        if isinstance(t, int):
            return t if t in (0, FAR) else t + FAR
        return jnp.where(lax.rem(t, FAR) == 0, t, t + FAR)

    def data_copy(d, t, s):
        part = pl.ds(s * ROWS, ROWS)
        return pltpu.make_async_remote_copy(
            src_ref=lists.at[place(d, t), part],
            dst_ref=lists.at[place(d, t + 1), part],
            send_sem=send_sem.at[d, t, s],
            recv_sem=recv_sem.at[d, t, s],
            device_id=ahead[d],
            device_id_type=MESH,
        )

    def aux_copy(d, t):
        return pltpu.make_async_remote_copy(
            src_ref=auxs.at[place(d, t)],
            dst_ref=auxs.at[place(d, t + 1)],
            send_sem=aux_send.at[d, t],
            recv_sem=aux_recv.at[d, t],
            device_id=ahead[d],
            device_id_type=MESH,
        )

    def off_copy(d, t):
        return pltpu.make_async_remote_copy(
            src_ref=offs.at[place(d, t)],
            dst_ref=offs.at[place(d, t + 1)],
            send_sem=off_send.at[d, t],
            recv_sem=off_recv.at[d, t],
            device_id=ahead[d],
            device_id_type=MESH,
        )

    def obl_copy(t):
        return pltpu.make_async_remote_copy(
            src_ref=obl.at[t],
            dst_ref=obl.at[t + 1],
            send_sem=obl_send.at[t],
            recv_sem=obl_recv.at[t],
            device_id=ahead[0],
            device_id_type=MESH,
        )

    def table_copy(i):
        return pltpu.make_async_copy(offs.at[i], tabs.at[i], tab_sem.at[i])

    barrier = pltpu.get_barrier_semaphore()
    for other in ahead:
        pl.semaphore_signal(barrier, inc=1, device_id=other, device_id_type=MESH)

    bins_in.wait()
    bins = bins_ref[...]
    keys = ((bins >> 14) << 14) + ((bins & 15) << 10) + ((bins >> 4) & 1023)
    key_rows[...] = keys
    digits[...] = jnp.zeros_like(digits)
    high, low = (keys >> 7).astype(F32), (keys & 127).astype(F32)
    for i in range(BLOCKS):
        lanes = slice(i * RB, (i + 1) * RB)
        digits[0:1, lanes] = high[i : i + 1, :]
        digits[1:2, lanes] = low[i : i + 1, :]
        key_cols[i * RB : (i + 1) * RB, :] = jnp.broadcast_to(key_rows[i : i + 1, :], (RB, RB)).T

    def rank_block(i, _):
        mine = jnp.broadcast_to(key_rows[pl.ds(i, 1), :], (RB, RB))
        total = jnp.zeros((RB, RB), jnp.int32)
        for j in range(BLOCKS):
            total += jnp.where(key_cols[j * RB : (j + 1) * RB, :] < mine, 1, 0)
        rank_rows[pl.ds(i, 1), :] = jnp.sum(total, axis=0, keepdims=True)
        return 0

    lax.fori_loop(0, BLOCKS, rank_block, 0)
    obl[0] = obl_in_ref[...].astype(F32)
    pl.semaphore_wait(barrier, 2)

    rows_in.wait()
    two_digits = digits[...].astype(BF16)
    for s in range(SUB):
        slots = lax.broadcasted_iota(jnp.int32, (ROWS, RB), 0) + s * ROWS
        for i in range(BLOCKS):
            onehot[:, i * RB : (i + 1) * RB] = jnp.where(
                slots == rank_rows[i : i + 1, :], 1.0, 0.0
            ).astype(BF16)
        taken = onehot[...]
        lists[0, s * ROWS : (s + 1) * ROWS, :] = jnp.dot(
            taken, rows_ref[...], preferred_element_type=F32
        ).astype(BF16)
        for d in (0, 1):
            data_copy(d, 0, s).start()
        found = lax.dot_general(
            two_digits, taken, (((1,), (1,)), ((), ())), preferred_element_type=F32
        )
        found = (found[0:1, :] * 128.0 + found[1:2, :]).astype(jnp.int32)
        per = ROWS // RB
        for i in range(per):
            now_aux[0, s * per + i : s * per + i + 1, :] = found[:, i * RB : (i + 1) * RB]
    starts = lax.broadcasted_iota(jnp.int32, (RB, RB), 1) * HALF
    total = jnp.zeros((RB, RB), jnp.int32)
    for j in range(BLOCKS):
        total += jnp.where(key_cols[j * RB : (j + 1) * RB, :] < starts, 1, 0)
    offsets = jnp.sum(total, axis=0, keepdims=True)
    offs[0] = offsets
    auxs[0] = now_aux[0].astype(jnp.int16)
    for d in (0, 1):
        aux_copy(d, 0).start()
        off_copy(d, 0).start()
    obl_copy(0).start()
    table_copy(0).start()
    table_copy(0).wait()

    slot_ids = lax.broadcasted_iota(jnp.int32, (HALF // 16, 16, RB), 0) * 16
    slot_ids = (slot_ids + lax.broadcasted_iota(jnp.int32, (HALF // 16, 16, RB), 1)).astype(jnp.int16)
    slots16[...] = slot_ids
    panel[...] = jnp.zeros_like(panel)

    def take(i, slot):
        def some(r, _):
            part = pl.ds(r * WIDTH, WIDTH)
            now[i, part, :] = lists[slot, part, :]
            return 0

        lax.fori_loop(0, PK // WIDTH, some, 0)
        now_aux[i] = auxs[slot].astype(jnp.int32)

    def place_rows(slots, count, g, _):
        placed = []
        for j in [g * count + i for i in range(count)]:
            b = jnp.where(j < BLOCKS, src * BLOCKS + j, (1 - src) * BLOCKS + rcv * 2 + j - BLOCKS)
            hits, packets = [], []
            for i, slot in enumerate(slots):
                k = jnp.clip(tabs[slot, 0, b] // RB, 0, (PK - WIN) // RB)
                for w in range(WIN // RB):
                    ids = now_aux[i, pl.ds(k + w, 1), :] - b * HALF
                    ids = jnp.broadcast_to(ids, (16, RB)).astype(jnp.int16)
                    hit = jnp.where(slots16[...] == ids[None], jnp.ones((), BF16), jnp.zeros((), BF16))
                    hits.append(hit.reshape(HALF, RB))
                rows = lists.at[FAR] if len(slots) == 1 else now.at[i]
                packets.append(rows[pl.ds(k * RB, WIN), :])
            found = packets[0] if len(packets) == 1 else jnp.concatenate(packets, axis=0)
            placed.append(
                jnp.dot(jnp.concatenate(hits, axis=1), found, preferred_element_type=F32).astype(BF16)
            )
        lanes = pl.ds(pl.multiple_of(g * (count * WIDTH), count * WIDTH), count * WIDTH)
        panel[:, lanes] += jnp.concatenate(placed, axis=1)
        return 0

    def step(t, _):
        slots = (t, place(1, t))
        take(0, slots[0])
        take(1, slots[1])

        @pl.when(t == 0)
        def _():
            now_aux[1] = jnp.full((BLOCKS, RB), -1, jnp.int32)

        def sub_block(s, _):
            groups = PANELS // PAIR
            lax.fori_loop(
                groups * s // SUB, groups * (s + 1) // SUB, functools.partial(place_rows, slots, PAIR), 0
            )

            @pl.when(t < FAR - 1)
            def _():
                for d in (0, 1):
                    data_copy(d, t, s).wait_recv()

                    @pl.when((t < FAR - 2) | ((s < SUB // 2) == (d == 0)))
                    def _(d=d):
                        data_copy(d, t + 1, s).start()

            return 0

        lax.fori_loop(0, SUB, sub_block, 0)

        @pl.when(t < FAR - 1)
        def _():
            for d in (0, 1):
                aux_copy(d, t).wait_recv()
                off_copy(d, t).wait_recv()
                table_copy(place(d, t + 1)).start()
            off_copy(0, t + 1).start()
            aux_copy(0, t + 1).start()

            @pl.when(t < FAR - 2)
            def _():
                off_copy(1, t + 1).start()
                aux_copy(1, t + 1).start()

            obl_copy(t).wait_recv()
            obl_copy(t + 1).start()
            for d in (0, 1):
                table_copy(place(d, t + 1)).wait()

        return 0

    lax.fori_loop(0, FAR, step, 0)

    def sent(t, _):
        for d in (0, 1):
            for s in range(SUB):

                @pl.when((t < FAR - 1) | ((s < SUB // 2) == (d == 0)))
                def _(d=d, s=s):
                    data_copy(d, t, s).wait_send()

        for copy in (off_copy, aux_copy):
            copy(0, t).wait_send()

            @pl.when(t < FAR - 1)
            def _(copy=copy):
                copy(1, t).wait_send()

        obl_copy(t).wait_send()
        return 0

    lax.fori_loop(0, FAR - 1, sent, 0)
    for s in range(SUB // 2):
        data_copy(0, FAR - 1, s).wait_recv()
    off_copy(0, FAR - 1).wait_recv()
    table_copy(FAR).start()
    aux_copy(0, FAR - 1).wait_recv()
    now_aux[0] = auxs[FAR].astype(jnp.int32)
    for s in range(SUB // 2, SUB):
        data_copy(1, FAR - 1, s).wait_recv()
    table_copy(FAR).wait()
    lax.fori_loop(0, PANELS // ONE, functools.partial(place_rows, (FAR,), ONE), 0)

    obl_copy(FAR - 1).wait_recv()
    wave_in.wait()
    w0, w1 = wave_ref[0], wave_ref[1]

    def filter_block(c, _):
        here = c // (BLOCKS // 2) == src
        lane = jnp.where(here, rcv * 2 * WIDTH, BLOCKS * WIDTH)
        block = lax.rem(c, BLOCKS // 2)
        data = panel[
            pl.ds(pl.multiple_of(block * RB, RB), RB),
            pl.ds(pl.multiple_of(lane, 2 * WIDTH), 2 * WIDTH),
        ].astype(F32)
        row = obl[jnp.where(here, 0, FAR), pl.ds(block, 1), :]
        scale = jnp.broadcast_to(row, (RB, RB)).T
        for i in range(2):
            re = data[:, i * WIDTH : i * WIDTH + RB]
            im = data[:, i * WIDTH + RB : (i + 1) * WIDTH]
            filt_re = ((w0 * re - w1 * im) * scale).astype(BF16)
            filt_im = ((w0 * im + w1 * re) * scale).astype(BF16)
            k = pl.multiple_of(c * WIDTH, WIDTH)
            left, right = slice(i * RB, (i + 1) * RB), slice(WIDTH + i * RB, WIDTH + (i + 1) * RB)
            weights[pl.ds(k, RB), left] = filt_re
            weights[pl.ds(k, RB), right] = filt_im
            weights[pl.ds(k + RB, RB), left] = -filt_im
            weights[pl.ds(k + RB, RB), right] = filt_re
        return 0

    lax.fori_loop(0, BLOCKS, filter_block, 0, unroll=4)

    tile = 512

    def product(m, _):
        part = pl.ds(pl.multiple_of(m * tile, tile), tile)
        for i in range(2):
            out_ref[i, part, :] = jnp.dot(
                panel[part, : BLOCKS * WIDTH],
                weights[:, i * WIDTH : (i + 1) * WIDTH],
                preferred_element_type=F32,
            )
        return 0

    lax.fori_loop(0, HALF // tile, product, 0)

    sent(FAR - 1, 0)


def on_device(packets, packet_bin, obliquity, wavelet):
    vmem, hbm = pl.BlockSpec(memory_space=pltpu.VMEM), pl.BlockSpec(memory_space=pltpu.HBM)
    dma = pltpu.SemaphoreType.DMA
    return pl.pallas_call(
        kernel,
        out_shape=jax.ShapeDtypeStruct((2, HALF, WIDTH), F32),
        in_specs=[hbm, hbm, vmem, hbm],
        out_specs=vmem,
        scratch_shapes=[
            pltpu.VMEM((PK, WIDTH), BF16),
            pltpu.VMEM((BLOCKS, RB), jnp.int32),
            pltpu.SMEM((2,), F32),
            pltpu.VMEM((GROUP, PK, WIDTH), BF16),
            pltpu.VMEM((GROUP, BLOCKS, RB), jnp.int16),
            pltpu.VMEM((GROUP, 1, RB), jnp.int32),
            pltpu.SMEM((GROUP, 1, RB), jnp.int32),
            pltpu.VMEM((2, PK, WIDTH), BF16),
            pltpu.VMEM((2, BLOCKS, RB), jnp.int32),
            pltpu.VMEM((HALF, PANELS * WIDTH), BF16),
            pltpu.VMEM((BLOCKS * WIDTH, 2 * WIDTH), BF16),
            pltpu.VMEM((HALF // 16, 16, RB), jnp.int16),
            pltpu.VMEM((ROWS, PK), BF16),
            pltpu.VMEM((PK, RB), jnp.int32),
            pltpu.VMEM((BLOCKS, RB), jnp.int32),
            pltpu.VMEM((BLOCKS, RB), jnp.int32),
            pltpu.VMEM((8, PK), F32),
            pltpu.VMEM((FAR + 1, 8, RB), F32),
            dma((2, FAR, SUB)),
            dma((2, FAR, SUB)),
            dma((2, FAR)),
            dma((2, FAR)),
            dma((2, FAR)),
            dma((2, FAR)),
            dma((FAR,)),
            dma((FAR,)),
            dma((GROUP,)),
            dma((3,)),
        ],
        compiler_params=pltpu.CompilerParams(
            collective_id=0, has_side_effects=True, vmem_limit_bytes=46 << 20
        ),
    )(
        pltpu.with_memory_space_constraint(packets, pltpu.HBM),
        pltpu.with_memory_space_constraint(packet_bin.reshape(BLOCKS, RB), pltpu.HBM),
        pltpu.with_memory_space_constraint(obliquity.reshape(8, RB), pltpu.HBM),
        pltpu.with_memory_space_constraint(wavelet, pltpu.HBM),
    )


def solution(mesh):
    return jax.shard_map(
        on_device,
        mesh=mesh,
        in_specs=(
            P(("freq", "src", "rcv"), None),
            P(("freq", "src", "rcv")),
            P(("freq", "src")),
            P("freq"),
        ),
        out_specs=P(None, ("freq", "src"), "rcv"),
        check_vma=False,
    )
```

```python
import functools

import jax
import jax.numpy as jnp
from jax import lax
from jax.experimental import pallas as pl
from jax.experimental.pallas import tpu as pltpu
from jax.sharding import PartitionSpec as P

MESH = pl.DeviceIdType.MESH
N = 2048
RB = 128
BLOCKS = N // RB
GROUP = 16
HALF = N // 2
PK = 2048
WIDTH = 2 * RB
SUB = 4
ROWS = PK // SUB
FAR = GROUP // 2
WIN = 384
PANELS = BLOCKS + 2
PAIR, ONE = 3, 6
BF16 = jnp.bfloat16
F32 = jnp.float32


def kernel(rows_hbm, bins_hbm, obl_in_ref, wave_hbm, out_ref, rows_ref, bins_ref, wave_ref, lists, auxs, offs, tabs,
           now, now_aux, panel, weights, slots16, key_cols, key_cols16, key_rows, rank_rows, digits, obl, send_sem,
           recv_sem, aux_send, aux_recv, off_send, off_recv, obl_sem, tab_sem, in_sem):
    bins_in = pltpu.make_async_copy(bins_hbm, bins_ref, in_sem.at[0])
    rows_in = pltpu.make_async_copy(rows_hbm, rows_ref, in_sem.at[1])
    wave_in = pltpu.make_async_copy(wave_hbm, wave_ref, in_sem.at[2])
    for copy in (bins_in, rows_in, wave_in):
        copy.start()
    src, rcv = lax.axis_index("src"), lax.axis_index("rcv")
    me = src * FAR + rcv

    def device(rank):
        rank = lax.rem(rank + GROUP, GROUP)
        return {"src": rank // FAR, "rcv": lax.rem(rank, FAR)}

    ahead = (device(me + 1), device(me - 1))

    def place(d, t):
        if d == 0:
            return t
        if isinstance(t, int):
            return t if t in (0, FAR) else t + FAR
        return jnp.where(lax.rem(t, FAR) == 0, t, t + FAR)

    def data_copy(d, t, s):
        part = pl.ds(s * ROWS, ROWS)
        return pltpu.make_async_remote_copy(
            src_ref=lists.at[place(d, t), part],
            dst_ref=lists.at[place(d, t + 1), part],
            send_sem=send_sem.at[d, t, s],
            recv_sem=recv_sem.at[d, t, s],
            device_id=ahead[d],
            device_id_type=MESH,
        )

    def aux_copy(d, t):
        return pltpu.make_async_remote_copy(
            src_ref=auxs.at[place(d, t)],
            dst_ref=auxs.at[place(d, t + 1)],
            send_sem=aux_send.at[d, t],
            recv_sem=aux_recv.at[d, t],
            device_id=ahead[d],
            device_id_type=MESH,
        )

    def off_copy(d, t):
        return pltpu.make_async_remote_copy(
            src_ref=offs.at[place(d, t)],
            dst_ref=offs.at[place(d, t + 1)],
            send_sem=off_send.at[d, t],
            recv_sem=off_recv.at[d, t],
            device_id=ahead[d],
            device_id_type=MESH,
        )

    def obl_copy(slot):
        return pltpu.make_async_remote_copy(
            src_ref=obl.at[slot],
            dst_ref=obl.at[1],
            send_sem=obl_sem.at[0],
            recv_sem=obl_sem.at[1],
            device_id=ahead[0],
            device_id_type=MESH,
        )

    def table_copy(i):
        return pltpu.make_async_copy(offs.at[i], tabs.at[i], tab_sem.at[i])

    barrier = pltpu.get_barrier_semaphore()
    for other in ahead:
        pl.semaphore_signal(barrier, inc=1, device_id=other, device_id_type=MESH)

    bins_in.wait()
    bins = bins_ref[...]
    keys = ((bins >> 14) << 14) + ((bins & 15) << 10) + ((bins >> 4) & 1023)
    key_rows[...] = keys
    digits[...] = jnp.zeros_like(digits)
    high, low = (keys >> 7).astype(F32), (keys & 127).astype(F32)
    for i in range(BLOCKS):
        lanes = slice(i * RB, (i + 1) * RB)
        digits[0:1, lanes] = high[i : i + 1, :]
        digits[1:2, lanes] = low[i : i + 1, :]
        column = jnp.broadcast_to(key_rows[i : i + 1, :], (RB, RB)).T
        key_cols[i * RB : (i + 1) * RB, :] = column
        key_cols16[i * RB : (i + 1) * RB, :] = column.astype(jnp.int16)

    def rank_block(i, _):
        mine = jnp.broadcast_to(key_rows[pl.ds(i, 1), :], (RB, RB)).astype(jnp.int16)
        total = jnp.zeros((RB, RB), jnp.int16)
        for j in range(BLOCKS):
            less = key_cols16[j * RB : (j + 1) * RB, :] < mine
            total += jnp.where(less, jnp.ones((), jnp.int16), jnp.zeros((), jnp.int16))
        rank_rows[pl.ds(i, 1), :] = jnp.sum(total.astype(jnp.int32), axis=0, keepdims=True)
        return 0

    lax.fori_loop(0, BLOCKS, rank_block, 0)
    obl[0] = obl_in_ref[...].astype(F32)
    pl.semaphore_wait(barrier, 2)

    rows_in.wait()
    onehot = panel.at[:ROWS, :PK]
    two_digits = digits[...].astype(BF16)
    for s in range(SUB):
        slots = lax.broadcasted_iota(jnp.int32, (ROWS, RB), 0) + s * ROWS
        for i in range(BLOCKS):
            onehot[:, i * RB : (i + 1) * RB] = jnp.where(
                slots == rank_rows[i : i + 1, :], 1.0, 0.0
            ).astype(BF16)
        taken = onehot[...]
        lists[0, s * ROWS : (s + 1) * ROWS, :] = jnp.dot(
            taken, rows_ref[...], preferred_element_type=F32
        ).astype(BF16)
        for d in (0, 1):
            data_copy(d, 0, s).start()
        found = lax.dot_general(
            two_digits, taken, (((1,), (1,)), ((), ())), preferred_element_type=F32
        )
        found = (found[0:1, :] * 128.0 + found[1:2, :]).astype(jnp.int32)
        per = ROWS // RB
        for i in range(per):
            now_aux[0, s * per + i : s * per + i + 1, :] = found[:, i * RB : (i + 1) * RB]
    starts = lax.broadcasted_iota(jnp.int32, (RB, RB), 1) * HALF
    total = jnp.zeros((RB, RB), jnp.int32)
    for j in range(BLOCKS):
        total += jnp.where(key_cols[j * RB : (j + 1) * RB, :] < starts, 1, 0)
    offsets = jnp.sum(total, axis=0, keepdims=True)
    offs[0] = offsets
    auxs[0] = now_aux[0].astype(jnp.int16)
    for d in (0, 1):
        aux_copy(d, 0).start()
        off_copy(d, 0).start()

    @pl.when(rcv == FAR - 1)
    def _():
        obl_copy(0).start()

    table_copy(0).start()
    table_copy(0).wait()

    slot_ids = lax.broadcasted_iota(jnp.int32, (HALF // 16, 16, RB), 0) * 16
    slot_ids = (slot_ids + lax.broadcasted_iota(jnp.int32, (HALF // 16, 16, RB), 1)).astype(jnp.int16)
    slots16[...] = slot_ids
    panel[...] = jnp.zeros_like(panel)

    def take(i, slot):
        def some(r, _):
            part = pl.ds(r * WIDTH, WIDTH)
            now[i, part, :] = lists[slot, part, :]
            return 0

        lax.fori_loop(0, PK // WIDTH, some, 0)
        now_aux[i] = auxs[slot].astype(jnp.int32)

    def found_rows(slots, j):
        b = jnp.where(j < BLOCKS, src * BLOCKS + j, (1 - src) * BLOCKS + rcv * 2 + j - BLOCKS)
        hits, packets = [], []
        for i, slot in enumerate(slots):
            k = jnp.clip(tabs[slot, 0, b] // RB, 0, (PK - WIN) // RB)
            for w in range(WIN // RB):
                ids = now_aux[i, pl.ds(k + w, 1), :] - b * HALF
                ids = jnp.broadcast_to(ids, (16, RB)).astype(jnp.int16)
                hit = jnp.where(slots16[...] == ids[None], jnp.ones((), BF16), jnp.zeros((), BF16))
                hits.append(hit.reshape(HALF, RB))
            rows = lists.at[FAR] if len(slots) == 1 else now.at[i]
            packets.append(rows[pl.ds(k * RB, WIN), :])
        found = packets[0] if len(packets) == 1 else jnp.concatenate(packets, axis=0)
        return jnp.dot(jnp.concatenate(hits, axis=1), found, preferred_element_type=F32).astype(BF16)

    def place_rows(slots, g, _):
        placed = [found_rows(slots, g * PAIR + i) for i in range(PAIR)]
        lanes = pl.ds(pl.multiple_of(g * (PAIR * WIDTH), PAIR * WIDTH), PAIR * WIDTH)
        panel[:, lanes] += jnp.concatenate(placed, axis=1)
        return 0

    def place_far(buckets):
        for j, rows in [(j, found_rows((FAR,), j)) for j in buckets]:
            panel[:, pl.ds(pl.multiple_of(j * WIDTH, WIDTH), WIDTH)] += rows

    def step(t, _):
        slots = (t, place(1, t))
        take(0, slots[0])
        take(1, slots[1])

        @pl.when(t == 0)
        def _():
            now_aux[1] = jnp.full((BLOCKS, RB), -1, jnp.int32)

        def sub_block(s, _):
            groups = PANELS // PAIR
            lax.fori_loop(groups * s // SUB, groups * (s + 1) // SUB, functools.partial(place_rows, slots), 0)

            @pl.when(t < FAR - 1)
            def _():
                for d in (0, 1):
                    data_copy(d, t, s).wait_recv()

                    @pl.when((t < FAR - 2) | ((s < SUB // 2) == (d == 0)))
                    def _(d=d):
                        data_copy(d, t + 1, s).start()

            return 0

        lax.fori_loop(0, SUB, sub_block, 0)

        @pl.when(t < FAR - 1)
        def _():
            for d in (0, 1):
                aux_copy(d, t).wait_recv()
                off_copy(d, t).wait_recv()
                table_copy(place(d, t + 1)).start()
            off_copy(0, t + 1).start()
            aux_copy(0, t + 1).start()

            @pl.when(t < FAR - 2)
            def _():
                off_copy(1, t + 1).start()
                aux_copy(1, t + 1).start()

            @pl.when(rcv == t)
            def _():
                obl_copy(1).wait_recv()
                obl_copy(1).start()

            for d in (0, 1):
                table_copy(place(d, t + 1)).wait()

        return 0

    lax.fori_loop(0, FAR, step, 0)

    def sent(t, _):
        for d in (0, 1):
            for s in range(SUB):

                @pl.when((t < FAR - 1) | ((s < SUB // 2) == (d == 0)))
                def _(d=d, s=s):
                    data_copy(d, t, s).wait_send()

        for copy in (off_copy, aux_copy):
            copy(0, t).wait_send()

            @pl.when(t < FAR - 1)
            def _(copy=copy):
                copy(1, t).wait_send()

        return 0

    lax.fori_loop(0, FAR - 1, sent, 0)
    for s in range(SUB // 2):
        data_copy(0, FAR - 1, s).wait_recv()
    off_copy(0, FAR - 1).wait_recv()
    table_copy(FAR).start()
    aux_copy(0, FAR - 1).wait_recv()
    now_aux[0] = auxs[FAR].astype(jnp.int32)
    for s in range(SUB // 2, SUB):
        data_copy(1, FAR - 1, s).wait_recv()
    table_copy(FAR).wait()

    @pl.when(rcv == FAR - 1)
    def _():
        obl_copy(1).wait_recv()

    wave_in.wait()
    w0, w1 = wave_ref[0], wave_ref[1]

    def filter_block(c):
        here = c // (BLOCKS // 2) == src
        lane = jnp.where(here, rcv * 2 * WIDTH, BLOCKS * WIDTH)
        block = lax.rem(c, BLOCKS // 2)
        data = panel[
            pl.ds(pl.multiple_of(block * RB, RB), RB),
            pl.ds(pl.multiple_of(lane, 2 * WIDTH), 2 * WIDTH),
        ].astype(F32)
        row = obl[jnp.where(here, 0, 1), pl.ds(block, 1), :]
        scale = jnp.broadcast_to(row, (RB, RB)).T
        for i in range(2):
            re = data[:, i * WIDTH : i * WIDTH + RB]
            im = data[:, i * WIDTH + RB : (i + 1) * WIDTH]
            filt_re = ((w0 * re - w1 * im) * scale).astype(BF16)
            filt_im = ((w0 * im + w1 * re) * scale).astype(BF16)
            k = pl.multiple_of(c * WIDTH, WIDTH)
            left, right = slice(i * RB, (i + 1) * RB), slice(WIDTH + i * RB, WIDTH + (i + 1) * RB)
            weights[pl.ds(k, RB), left] = filt_re
            weights[pl.ds(k, RB), right] = filt_im
            weights[pl.ds(k + RB, RB), left] = -filt_im
            weights[pl.ds(k + RB, RB), right] = filt_re

    place_far([BLOCKS, BLOCKS + 1] + [lax.rem(rcv * 2 + i, BLOCKS) for i in range(ONE - 2)])

    def far_and_filter(g, _):
        for i in range(BLOCKS // 2):
            filter_block(g * (BLOCKS // 2) + i)
        place_far([lax.rem(rcv * 2 + (g + 1) * ONE - 2 + i, BLOCKS) for i in range(ONE)])
        return 0

    lax.fori_loop(0, PANELS // ONE - 1, far_and_filter, 0)

    tile = 512

    def product(m, _):
        part = pl.ds(pl.multiple_of(m * tile, tile), tile)
        for i in range(2):
            out_ref[i, part, :] = jnp.dot(
                panel[part, : BLOCKS * WIDTH],
                weights[:, i * WIDTH : (i + 1) * WIDTH],
                preferred_element_type=F32,
            )
        return 0

    lax.fori_loop(0, HALF // tile, product, 0)

    sent(FAR - 1, 0)
    obl_copy(0).wait_send()


def on_device(packets, packet_bin, obliquity, wavelet):
    vmem, hbm = pl.BlockSpec(memory_space=pltpu.VMEM), pl.BlockSpec(memory_space=pltpu.HBM)
    dma = pltpu.SemaphoreType.DMA
    return pl.pallas_call(
        kernel,
        out_shape=jax.ShapeDtypeStruct((2, HALF, WIDTH), F32),
        in_specs=[hbm, hbm, vmem, hbm],
        out_specs=vmem,
        scratch_shapes=[
            pltpu.VMEM((PK, WIDTH), BF16),
            pltpu.VMEM((BLOCKS, RB), jnp.int32),
            pltpu.SMEM((2,), F32),
            pltpu.VMEM((GROUP, PK, WIDTH), BF16),
            pltpu.VMEM((GROUP, BLOCKS, RB), jnp.int16),
            pltpu.VMEM((GROUP, 1, RB), jnp.int32),
            pltpu.SMEM((GROUP, 1, RB), jnp.int32),
            pltpu.VMEM((2, PK, WIDTH), BF16),
            pltpu.VMEM((2, BLOCKS, RB), jnp.int32),
            pltpu.VMEM((HALF, PANELS * WIDTH), BF16),
            pltpu.VMEM((BLOCKS * WIDTH, 2 * WIDTH), BF16),
            pltpu.VMEM((HALF // 16, 16, RB), jnp.int16),
            pltpu.VMEM((PK, RB), jnp.int32),
            pltpu.VMEM((PK, RB), jnp.int16),
            pltpu.VMEM((BLOCKS, RB), jnp.int32),
            pltpu.VMEM((BLOCKS, RB), jnp.int32),
            pltpu.VMEM((8, PK), F32),
            pltpu.VMEM((2, 8, RB), F32),
            dma((2, FAR, SUB)),
            dma((2, FAR, SUB)),
            dma((2, FAR)),
            dma((2, FAR)),
            dma((2, FAR)),
            dma((2, FAR)),
            dma((2,)),
            dma((GROUP,)),
            dma((3,)),
        ],
        compiler_params=pltpu.CompilerParams(
            collective_id=0, has_side_effects=True, vmem_limit_bytes=48 << 20
        ),
    )(
        pltpu.with_memory_space_constraint(packets, pltpu.HBM),
        pltpu.with_memory_space_constraint(packet_bin.reshape(BLOCKS, RB), pltpu.HBM),
        pltpu.with_memory_space_constraint(obliquity.reshape(8, RB), pltpu.HBM),
        pltpu.with_memory_space_constraint(wavelet, pltpu.HBM),
    )


def solution(mesh):
    return jax.shard_map(
        on_device,
        mesh=mesh,
        in_specs=(
            P(("freq", "src", "rcv"), None),
            P(("freq", "src", "rcv")),
            P(("freq", "src")),
            P("freq"),
        ),
        out_specs=P(None, ("freq", "src"), "rcv"),
        check_vma=False,
    )
```

```python
import functools

import jax
import jax.numpy as jnp
from jax import lax
from jax.experimental import pallas as pl
from jax.experimental.pallas import tpu as pltpu
from jax.sharding import PartitionSpec as P

MESH = pl.DeviceIdType.MESH
N = 2048
RB = 128
BLOCKS = N // RB
GROUP = 16
HALF = N // 2
PK = 2048
WIDTH = 2 * RB
SUB = 4
ROWS = PK // SUB
FAR = GROUP // 2
WIN = 384
PANELS = BLOCKS + 2
PAIR, ONE = 3, 6
BF16 = jnp.bfloat16
F32 = jnp.float32


def kernel(rows_hbm, bins_hbm, obl_in_ref, wave_hbm, out_ref, rows_ref, bins_ref, wave_ref, lists, auxs, offs, tabs,
           now, now_aux, panel, weights, slots16, key_cols, key_cols16, key_rows, rank_rows, digits, obl, send_sem,
           recv_sem, aux_send, aux_recv, off_send, off_recv, obl_sem, tab_sem, in_sem):
    bins_in = pltpu.make_async_copy(bins_hbm, bins_ref, in_sem.at[0])
    rows_in = pltpu.make_async_copy(rows_hbm, rows_ref, in_sem.at[1])
    wave_in = pltpu.make_async_copy(wave_hbm, wave_ref, in_sem.at[2])
    for copy in (bins_in, rows_in, wave_in):
        copy.start()
    src, rcv = lax.axis_index("src"), lax.axis_index("rcv")
    me = src * FAR + rcv

    def device(rank):
        rank = lax.rem(rank + GROUP, GROUP)
        return {"src": rank // FAR, "rcv": lax.rem(rank, FAR)}

    ahead = (device(me + 1), device(me - 1))

    def place(d, t):
        if d == 0:
            return t
        if isinstance(t, int):
            return t if t in (0, FAR) else t + FAR
        return jnp.where(lax.rem(t, FAR) == 0, t, t + FAR)

    def data_copy(d, t, s):
        part = pl.ds(s * ROWS, ROWS)
        return pltpu.make_async_remote_copy(
            src_ref=lists.at[place(d, t), part],
            dst_ref=lists.at[place(d, t + 1), part],
            send_sem=send_sem.at[d, t, s],
            recv_sem=recv_sem.at[d, t, s],
            device_id=ahead[d],
            device_id_type=MESH,
        )

    def aux_copy(d, t):
        return pltpu.make_async_remote_copy(
            src_ref=auxs.at[place(d, t)],
            dst_ref=auxs.at[place(d, t + 1)],
            send_sem=aux_send.at[d, t],
            recv_sem=aux_recv.at[d, t],
            device_id=ahead[d],
            device_id_type=MESH,
        )

    def off_copy(d, t):
        return pltpu.make_async_remote_copy(
            src_ref=offs.at[place(d, t)],
            dst_ref=offs.at[place(d, t + 1)],
            send_sem=off_send.at[d, t],
            recv_sem=off_recv.at[d, t],
            device_id=ahead[d],
            device_id_type=MESH,
        )

    def obl_copy(slot):
        return pltpu.make_async_remote_copy(
            src_ref=obl.at[slot],
            dst_ref=obl.at[1],
            send_sem=obl_sem.at[0],
            recv_sem=obl_sem.at[1],
            device_id=ahead[0],
            device_id_type=MESH,
        )

    def table_copy(i):
        return pltpu.make_async_copy(offs.at[i], tabs.at[i], tab_sem.at[i])

    barrier = pltpu.get_barrier_semaphore()
    for other in ahead:
        pl.semaphore_signal(barrier, inc=1, device_id=other, device_id_type=MESH)

    bins_in.wait()
    bins = bins_ref[...]
    keys = ((bins >> 14) << 14) + ((bins & 15) << 10) + ((bins >> 4) & 1023)
    key_rows[...] = keys
    digits[...] = jnp.zeros_like(digits)
    high, low = (keys >> 7).astype(F32), (keys & 127).astype(F32)
    for i in range(BLOCKS):
        lanes = slice(i * RB, (i + 1) * RB)
        digits[0:1, lanes] = high[i : i + 1, :]
        digits[1:2, lanes] = low[i : i + 1, :]
        column = jnp.broadcast_to(key_rows[i : i + 1, :], (RB, RB)).T
        key_cols[i * RB : (i + 1) * RB, :] = column
        key_cols16[i * RB : (i + 1) * RB, :] = column.astype(jnp.int16)

    def rank_block(i, _):
        mine = jnp.broadcast_to(key_rows[pl.ds(i, 1), :], (RB, RB)).astype(jnp.int16)
        total = jnp.zeros((RB, RB), jnp.int16)
        for j in range(BLOCKS):
            less = key_cols16[j * RB : (j + 1) * RB, :] < mine
            total += jnp.where(less, jnp.ones((), jnp.int16), jnp.zeros((), jnp.int16))
        rank_rows[pl.ds(i, 1), :] = jnp.sum(total.astype(jnp.int32), axis=0, keepdims=True)
        return 0

    lax.fori_loop(0, BLOCKS, rank_block, 0)
    obl[0] = obl_in_ref[...].astype(F32)
    pl.semaphore_wait(barrier, 2)

    rows_in.wait()
    onehot = panel.at[:ROWS, :PK]
    two_digits = digits[...].astype(BF16)
    for s in range(SUB):
        slots = lax.broadcasted_iota(jnp.int32, (ROWS, RB), 0) + s * ROWS
        for i in range(BLOCKS):
            onehot[:, i * RB : (i + 1) * RB] = jnp.where(
                slots == rank_rows[i : i + 1, :], 1.0, 0.0
            ).astype(BF16)
        taken = onehot[...]
        lists[0, s * ROWS : (s + 1) * ROWS, :] = jnp.dot(
            taken, rows_ref[...], preferred_element_type=F32
        ).astype(BF16)
        for d in (0, 1):
            data_copy(d, 0, s).start()
        found = lax.dot_general(
            two_digits, taken, (((1,), (1,)), ((), ())), preferred_element_type=F32
        )
        found = (found[0:1, :] * 128.0 + found[1:2, :]).astype(jnp.int32)
        per = ROWS // RB
        for i in range(per):
            now_aux[0, s * per + i : s * per + i + 1, :] = found[:, i * RB : (i + 1) * RB]
    starts = lax.broadcasted_iota(jnp.int32, (RB, RB), 1) * HALF
    total = jnp.zeros((RB, RB), jnp.int32)
    for j in range(BLOCKS):
        total += jnp.where(key_cols[j * RB : (j + 1) * RB, :] < starts, 1, 0)
    offsets = jnp.sum(total, axis=0, keepdims=True)
    offs[0] = offsets
    auxs[0] = now_aux[0].astype(jnp.int16)
    for d in (0, 1):
        aux_copy(d, 0).start()
        off_copy(d, 0).start()

    @pl.when(rcv == FAR - 1)
    def _():
        obl_copy(0).start()

    table_copy(0).start()
    table_copy(0).wait()

    slot_ids = lax.broadcasted_iota(jnp.int32, (HALF // 16, 16, RB), 0) * 16
    slot_ids = (slot_ids + lax.broadcasted_iota(jnp.int32, (HALF // 16, 16, RB), 1)).astype(jnp.int16)
    slots16[...] = slot_ids
    panel[...] = jnp.zeros_like(panel)

    def take(i, slot):
        def some(r, _):
            part = pl.ds(r * WIDTH, WIDTH)
            now[i, part, :] = lists[slot, part, :]
            return 0

        lax.fori_loop(0, PK // WIDTH, some, 0)
        now_aux[i] = auxs[slot].astype(jnp.int32)

    def found_rows(slots, j):
        b = jnp.where(j < BLOCKS, src * BLOCKS + j, (1 - src) * BLOCKS + rcv * 2 + j - BLOCKS)
        hits, packets = [], []
        for i, slot in enumerate(slots):
            k = jnp.clip(tabs[slot, 0, b] // RB, 0, (PK - WIN) // RB)
            for w in range(WIN // RB):
                ids = now_aux[i, pl.ds(k + w, 1), :] - b * HALF
                ids = jnp.broadcast_to(ids, (16, RB)).astype(jnp.int16)
                hit = jnp.where(slots16[...] == ids[None], jnp.ones((), BF16), jnp.zeros((), BF16))
                hits.append(hit.reshape(HALF, RB))
            rows = lists.at[FAR] if len(slots) == 1 else now.at[i]
            packets.append(rows[pl.ds(k * RB, WIN), :])
        found = packets[0] if len(packets) == 1 else jnp.concatenate(packets, axis=0)
        return jnp.dot(jnp.concatenate(hits, axis=1), found, preferred_element_type=F32).astype(BF16)

    def place_rows(slots, g, _):
        placed = [found_rows(slots, g * PAIR + i) for i in range(PAIR)]
        lanes = pl.ds(pl.multiple_of(g * (PAIR * WIDTH), PAIR * WIDTH), PAIR * WIDTH)
        panel[:, lanes] += jnp.concatenate(placed, axis=1)
        return 0

    def place_far(buckets):
        for j, rows in [(j, found_rows((FAR,), j)) for j in buckets]:
            panel[:, pl.ds(pl.multiple_of(j * WIDTH, WIDTH), WIDTH)] += rows

    def sent(t, _):
        for d in (0, 1):
            for s in range(SUB):

                @pl.when((t < FAR - 1) | ((s < SUB // 2) == (d == 0)))
                def _(d=d, s=s):
                    data_copy(d, t, s).wait_send()

        for copy in (off_copy, aux_copy):
            copy(0, t).wait_send()

            @pl.when(t < FAR - 1)
            def _(copy=copy):
                copy(1, t).wait_send()

        return 0

    def step(t, _):
        slots = (t, place(1, t))
        take(0, slots[0])
        take(1, slots[1])

        @pl.when(t == 0)
        def _():
            now_aux[1] = jnp.full((BLOCKS, RB), -1, jnp.int32)

        def sub_block(s, _):
            groups = PANELS // PAIR
            lax.fori_loop(groups * s // SUB, groups * (s + 1) // SUB, functools.partial(place_rows, slots), 0)

            @pl.when(t < FAR - 1)
            def _():
                for d in (0, 1):
                    data_copy(d, t, s).wait_recv()

                    @pl.when((t < FAR - 2) | ((s < SUB // 2) == (d == 0)))
                    def _(d=d):
                        data_copy(d, t + 1, s).start()

            return 0

        lax.fori_loop(0, SUB, sub_block, 0)

        @pl.when((t > 0) & (t < FAR - 1))
        def _():
            sent(t - 1, 0)

        @pl.when(t < FAR - 1)
        def _():
            for d in (0, 1):
                aux_copy(d, t).wait_recv()
                off_copy(d, t).wait_recv()
                table_copy(place(d, t + 1)).start()
            off_copy(0, t + 1).start()
            aux_copy(0, t + 1).start()

            @pl.when(t < FAR - 2)
            def _():
                off_copy(1, t + 1).start()
                aux_copy(1, t + 1).start()

            @pl.when(rcv == t)
            def _():
                obl_copy(1).wait_recv()
                obl_copy(1).start()

            for d in (0, 1):
                table_copy(place(d, t + 1)).wait()

        return 0

    lax.fori_loop(0, FAR, step, 0)

    for s in range(SUB // 2):
        data_copy(0, FAR - 1, s).wait_recv()
    off_copy(0, FAR - 1).wait_recv()
    table_copy(FAR).start()
    aux_copy(0, FAR - 1).wait_recv()
    now_aux[0] = auxs[FAR].astype(jnp.int32)
    for s in range(SUB // 2, SUB):
        data_copy(1, FAR - 1, s).wait_recv()
    table_copy(FAR).wait()

    @pl.when(rcv == FAR - 1)
    def _():
        obl_copy(1).wait_recv()

    wave_in.wait()
    w0, w1 = wave_ref[0], wave_ref[1]

    def filter_block(c):
        here = c // (BLOCKS // 2) == src
        lane = jnp.where(here, rcv * 2 * WIDTH, BLOCKS * WIDTH)
        block = lax.rem(c, BLOCKS // 2)
        data = panel[
            pl.ds(pl.multiple_of(block * RB, RB), RB),
            pl.ds(pl.multiple_of(lane, 2 * WIDTH), 2 * WIDTH),
        ].astype(F32)
        row = obl[jnp.where(here, 0, 1), pl.ds(block, 1), :]
        scale = jnp.broadcast_to(row, (RB, RB)).T
        for i in range(2):
            re = data[:, i * WIDTH : i * WIDTH + RB]
            im = data[:, i * WIDTH + RB : (i + 1) * WIDTH]
            filt_re = ((w0 * re - w1 * im) * scale).astype(BF16)
            filt_im = ((w0 * im + w1 * re) * scale).astype(BF16)
            k = pl.multiple_of(c * WIDTH, WIDTH)
            left, right = slice(i * RB, (i + 1) * RB), slice(WIDTH + i * RB, WIDTH + (i + 1) * RB)
            weights[pl.ds(k, RB), left] = filt_re
            weights[pl.ds(k, RB), right] = filt_im
            weights[pl.ds(k + RB, RB), left] = -filt_im
            weights[pl.ds(k + RB, RB), right] = filt_re

    place_far([BLOCKS, BLOCKS + 1] + [lax.rem(rcv * 2 + i, BLOCKS) for i in range(ONE - 2)])

    def far_and_filter(g, _):
        for i in range(BLOCKS // 2):
            filter_block(g * (BLOCKS // 2) + i)
        place_far([lax.rem(rcv * 2 + (g + 1) * ONE - 2 + i, BLOCKS) for i in range(ONE)])
        return 0

    lax.fori_loop(0, PANELS // ONE - 1, far_and_filter, 0)

    tile = 512

    def product(m, _):
        part = pl.ds(pl.multiple_of(m * tile, tile), tile)
        for i in range(2):
            out_ref[i, part, :] = jnp.dot(
                panel[part, : BLOCKS * WIDTH],
                weights[:, i * WIDTH : (i + 1) * WIDTH],
                preferred_element_type=F32,
            )
        return 0

    lax.fori_loop(0, HALF // tile, product, 0)

    lax.fori_loop(FAR - 2, FAR, sent, 0)
    obl_copy(0).wait_send()


def on_device(packets, packet_bin, obliquity, wavelet):
    vmem, hbm = pl.BlockSpec(memory_space=pltpu.VMEM), pl.BlockSpec(memory_space=pltpu.HBM)
    dma = pltpu.SemaphoreType.DMA
    return pl.pallas_call(
        kernel,
        out_shape=jax.ShapeDtypeStruct((2, HALF, WIDTH), F32),
        in_specs=[hbm, hbm, vmem, hbm],
        out_specs=vmem,
        scratch_shapes=[
            pltpu.VMEM((PK, WIDTH), BF16),
            pltpu.VMEM((BLOCKS, RB), jnp.int32),
            pltpu.SMEM((2,), F32),
            pltpu.VMEM((GROUP, PK, WIDTH), BF16),
            pltpu.VMEM((GROUP, BLOCKS, RB), jnp.int16),
            pltpu.VMEM((GROUP, 1, RB), jnp.int32),
            pltpu.SMEM((GROUP, 1, RB), jnp.int32),
            pltpu.VMEM((2, PK, WIDTH), BF16),
            pltpu.VMEM((2, BLOCKS, RB), jnp.int32),
            pltpu.VMEM((HALF, PANELS * WIDTH), BF16),
            pltpu.VMEM((BLOCKS * WIDTH, 2 * WIDTH), BF16),
            pltpu.VMEM((HALF // 16, 16, RB), jnp.int16),
            pltpu.VMEM((PK, RB), jnp.int32),
            pltpu.VMEM((PK, RB), jnp.int16),
            pltpu.VMEM((BLOCKS, RB), jnp.int32),
            pltpu.VMEM((BLOCKS, RB), jnp.int32),
            pltpu.VMEM((8, PK), F32),
            pltpu.VMEM((2, 8, RB), F32),
            dma((2, FAR, SUB)),
            dma((2, FAR, SUB)),
            dma((2, FAR)),
            dma((2, FAR)),
            dma((2, FAR)),
            dma((2, FAR)),
            dma((2,)),
            dma((GROUP,)),
            dma((3,)),
        ],
        compiler_params=pltpu.CompilerParams(
            collective_id=0, has_side_effects=True, vmem_limit_bytes=48 << 20
        ),
    )(
        pltpu.with_memory_space_constraint(packets, pltpu.HBM),
        pltpu.with_memory_space_constraint(packet_bin.reshape(BLOCKS, RB), pltpu.HBM),
        pltpu.with_memory_space_constraint(obliquity.reshape(8, RB), pltpu.HBM),
        pltpu.with_memory_space_constraint(wavelet, pltpu.HBM),
    )


def solution(mesh):
    return jax.shard_map(
        on_device,
        mesh=mesh,
        in_specs=(
            P(("freq", "src", "rcv"), None),
            P(("freq", "src", "rcv")),
            P(("freq", "src")),
            P("freq"),
        ),
        out_specs=P(None, ("freq", "src"), "rcv"),
        check_vma=False,
    )
```
